512 devices in a mesh: dp: 8 (over z), tensor: 4 (over y_lo, core), grid: 16 (over y_hi, x).
Axes of the slice: x: 4, y: 8 (y_hi: 4, y_lo: 2; y = y_hi * 2 + y_lo), z: 8, core: 2. Of those that a mesh axis runs over, the one named last changes fastest.
Arguments:
- tokens: bfloat16 [6144, 8192], P('dp', 'grid'), may hold values from -6 to 6
- cotangents: bfloat16 [2, 6144, 1024], P(None, 'dp', 'tensor'), may hold values from -0.015625 to 0.015625
- left_stat: float32 [2, 8192, 8192], P(None, ('dp', 'tensor'), 'grid'), may hold values from -6 to 6
- right_stat: float32 [2, 1024, 1024], P(None, ('dp', 'tensor'), 'grid'), may hold values from -6 to 6
- left_root: bfloat16 [2, 8192, 8192], P(None, ('dp', 'tensor'), 'grid'), may hold values from -0.3125 to 0.3125
- right_root: bfloat16 [2, 1024, 1024], P(None, 'grid'), as said below
- momentum: float32 [2, 8192, 1024], P(None, ('dp', 'tensor', 'grid')), may hold values from -6 to 6
Outputs:
- new_left: float32 [2, 8192, 8192], P(None, ('dp', 'tensor'), 'grid')
- new_right: float32 [2, 1024, 1024], P(None, ('dp', 'tensor'), 'grid')
- new_momentum: float32 [2, 8192, 1024], P(None, ('dp', 'tensor', 'grid'))
The draws below stay inside these ranges and needn't reach their ends.
Inputs may be any that keep to these rules, and one draw needn't show every extreme that they name: `right_root`: each of the two factors is exactly symmetric.
All inputs are finite; a program needn't handle non-finite values.
Results may differ from the reference program's by a relative error of at most 0.0023.
Values may be sent and summed in bfloat16 or wider, within the bound.
A program may use at most 64 MiB of HBM per device.

```python
import math
import jax
import jax.numpy as jnp
from jax import lax

D = 8192
KV = 1024
TOKENS = 6144


def draw_right_root(key, part):
    raw = jax.random.normal(key, (2, KV, KV), jnp.float32)
    symmetric = (raw + jnp.swapaxes(raw, 1, 2)) * (0.35 / math.sqrt(KV))
    return (symmetric + jnp.eye(KV, dtype=jnp.float32)).astype(jnp.bfloat16)


def block_scale(stream_key, extent, cuts, low, high):
    factor_of, own = 1.0, jax.random.fold_in(stream_key, 6)
    for position, blocks in cuts:
        heights = jnp.exp(jax.random.uniform(jax.random.fold_in(own, position), (blocks,), jnp.float32, low / len(cuts), high / len(cuts)))
        factor_of = factor_of * jnp.repeat(heights, extent[position] // blocks).reshape([-1 if axis == position else 1 for axis in range(len(extent))])
    return factor_of


def noise(key, extent, scale, most, cuts=(), held_as=jnp.bfloat16):
    drawn = scale * jax.random.normal(key, extent, jnp.float32)
    if cuts:
        drawn = drawn * block_scale(key, extent, cuts, -0.22, 0.18)
    return jnp.clip(drawn, -most, most).astype(held_as)


def setup_inputs(seed: int = 0) -> dict:
    arg_keys = jax.random.split(jax.random.key(seed), 8)
    return {
        "tokens": noise(arg_keys[0], (TOKENS, D), 1.0, 6.0, ((0, 8), (1, 16))),
        "cotangents": noise(arg_keys[1], (2, TOKENS, KV), (25 * TOKENS) ** -0.5, 0.015625, ((1, 8), (2, 4))),
        "left_stat": noise(arg_keys[2], (2, D, D), 1.0, 6.0, ((1, 32), (2, 16)), jnp.float32),
        "right_stat": noise(arg_keys[3], (2, KV, KV), 1.0, 6.0, ((1, 32), (2, 16)), jnp.float32),
        "left_root": noise(arg_keys[4], (2, D, D), (D // 25) ** -0.5, 0.3125, ((1, 32), (2, 16))),
        "right_root": draw_right_root(jax.random.fold_in(arg_keys[7], 71), 0),
        "momentum": noise(arg_keys[6], (2, D, KV), 1.0, 6.0, ((1, 512),), jnp.float32),
    }


stat_decay = 0.9
momentum_decay = 0.9


def reference(tokens, cotangents, left_stat, right_stat, left_root, right_root, momentum):
    left_list = []
    right_list = []
    moment_list = []
    for project in range(2):
        gradient = jnp.dot(tokens.T, cotangents[project], preferred_element_type=jnp.float32)
        rounded = gradient.astype(jnp.bfloat16)
        gram_left = jnp.dot(rounded, rounded.T, preferred_element_type=jnp.float32)
        gram_right = jnp.dot(rounded.T, rounded, preferred_element_type=jnp.float32)
        left_list.append(stat_decay * left_stat[project] + (1.0 - stat_decay) * gram_left)
        right_list.append(stat_decay * right_stat[project] + (1.0 - stat_decay) * gram_right)
        applied = jnp.dot(left_root[project], rounded, preferred_element_type=jnp.float32)
        factor = right_root[project].astype(jnp.float32)
        update = jnp.dot(applied, factor, precision=lax.Precision.HIGHEST, preferred_element_type=jnp.float32)
        moment_list.append(momentum_decay * momentum[project] + update)
    return jnp.stack(left_list), jnp.stack(right_list), jnp.stack(moment_list)
```

```python
import jax
import jax.numpy as jnp
from jax import lax
from jax.experimental import pallas as pl
from jax.experimental.pallas import tpu as pltpu
from jax.sharding import PartitionSpec as P

MESH = pl.DeviceIdType.MESH
f32, bf16 = jnp.float32, jnp.bfloat16

stat_decay = 0.9
momentum_decay = 0.9

NZ, NT, NG, NX, NY = 8, 4, 16, 4, 4
Z_ORDER = (1, 7, 2, 6, 3, 5, 4)


def remote(src, dst, send_sem, recv_sem, device):
    return pltpu.make_async_remote_copy(
        src_ref=src, dst_ref=dst, send_sem=send_sem, recv_sem=recv_sem,
        device_id=device, device_id_type=MESH,
    )


def kernel(
    tokens, cots, left_root, right_root,
    gram_left, gram_right, update,
    part, ring, gbuf, gsub, r1, r2, r3, rbuf, rr,
    xs, xr, ax, ys, yr, uf, ur, gr_tmp, gs32, gs, gr,
    ring_send, ring_recv, ag_send, ag_recv, sib_send, sib_recv, yl_send, yl_recv,
    sib2_send, sib2_recv, x_send, x_recv, pair_send, pair_recv,
):
    d, t, g = lax.axis_index("dp"), lax.axis_index("tensor"), lax.axis_index("grid")
    y, x = g // NX, g % NX
    core, y_lo = t % 2, t // 2
    sibling = y_lo * 2 + (1 - core)
    partner = (1 - y_lo) * 2 + core
    learner = d * NT + t

    barrier = pltpu.get_barrier_semaphore()

    @pl.loop(1, NZ * NT)
    def _(k):
        other = (learner + k) % (NZ * NT)
        pl.semaphore_signal(barrier, inc=1, device_id=(other // NT, other % NT, g), device_id_type=MESH)

    @pl.loop(1, NG)
    def _(k):
        pl.semaphore_signal(barrier, inc=1, device_id=(d, t, (g + k) % NG), device_id_type=MESH)

    turned = tokens[...].T
    for p in range(2):
        whole = jnp.dot(turned, cots[p], preferred_element_type=f32)
        for z in range(NZ):
            part[z, p] = whole[z * 64 : z * 64 + 64]

    pl.semaphore_wait(barrier, NZ * NT - 1 + NG - 1)

    sent = []

    def go(copy):
        copy.start()
        sent.append(copy)

    up, down = ((d + 1) % NZ, t, g), ((d + NZ - 1) % NZ, t, g)

    def length(way, p):
        return 4 if way == p else 3

    for step in range(4):
        for p in range(2):
            for way in range(2):
                n = length(way, p)
                if step >= n:
                    continue
                e = (d + n - step) % NZ if way == 0 else (d + NZ - n + step) % NZ
                if step == 0:
                    src = part.at[e, p]
                else:
                    slot = ring.at[way, p, step - 1]
                    remote(slot, slot, ring_send.at[way, p, step - 1], ring_recv.at[way, p, step - 1], up).wait_recv()
                    ring[way, p, step - 1] = ring[way, p, step - 1] + part[e, p]
                    src = slot
                go(remote(src, ring.at[way, p, step], ring_send.at[way, p, step], ring_recv.at[way, p, step],
                          up if way == 0 else down))
        if step == 0:
            @pl.loop(0, NY)
            def _(q):
                @pl.when(jnp.logical_or(q != y, x != y))
                def _():
                    remote(right_root.at[core], rr.at[core, pl.ds(x * 64, 64)], pair_send.at[0], pair_recv.at[0],
                           (d, t, q * NX + y)).start()

            @pl.when(x == y)
            def _():
                rr[core, pl.ds(x * 64, 64), :] = right_root[core]

    for p in range(2):
        total = part[d, p]
        for way in range(2):
            n = length(way, p)
            slot = ring.at[way, p, n - 1]
            remote(slot, slot, ring_send.at[way, p, n - 1], ring_recv.at[way, p, n - 1], up).wait_recv()
            total = total + ring[way, p, n - 1]
        piece = total.astype(bf16)
        gbuf[p, t, pl.ds(d * 64, 64), :] = piece
        for a in range(4):
            for c in range(2):
                gsub[p * 8 + a * 2 + c] = piece[a * 16 : a * 16 + 16, c * 128 : c * 128 + 128]

    def rows_of(tensor, k):
        return gbuf.at[:, tensor, pl.ds(((d + NZ - k) % NZ) * 64, 64), :]

    for k in Z_ORDER:
        go(remote(rows_of(t, 0), rows_of(t, 0), ag_send.at[k], ag_recv.at[k], ((d + k) % NZ, t, g)))

    def pass_on(k):
        go(remote(rows_of(t, k), rows_of(t, k), yl_send.at[k], yl_recv.at[k], (d, partner, g)))
        go(remote(rows_of(t, k), rows_of(t, k), sib_send.at[k], sib_recv.at[k], (d, sibling, g)))

    def pass_again(k):
        here = rows_of(partner, k)
        remote(here, here, yl_send.at[k], yl_recv.at[k], (d, partner, g)).wait_recv()
        go(remote(here, here, sib2_send.at[k], sib2_recv.at[k], (d, sibling, g)))

    def arrived(k):
        here = rows_of(t, k)
        remote(here, here, ag_send.at[k], ag_recv.at[k], (d, partner, g)).wait_recv()

    pass_on(0)

    @pl.loop(1, NG)
    def _(k):
        to = (g + k) % NG
        remote(gsub.at[to], r1.at[g], pair_send.at[1], pair_recv.at[1], (d, t, to)).start()

    r1[g] = gsub[g]

    def many(ref, s):
        return remote(ref, ref, pair_send.at[s], pair_recv.at[s], (d, sibling, g))

    for k in (1, 7):
        arrived(k)
        pass_on(k)
    pass_again(0)

    mine = d // 4 == core
    many(r1.at[pl.ds(0, NG - 1)], 1).wait_recv()

    @pl.loop(0, NG)
    def _(b):
        to_z, to_t = b // 2, (b % 2) * 2 + d // 4
        @pl.when(jnp.logical_or(to_z != d, to_t != t))
        def _():
            remote(r1.at[b], r2.at[(d % 4) * NT + t], pair_send.at[2], pair_recv.at[2], (to_z, to_t, g)).start()

    @pl.when(mine)
    def _():
        r2[(d % 4) * NT + t] = r1[2 * d + y_lo]

    for k in (2, 6):
        arrived(k)
        pass_on(k)
    for k in (1, 7):
        pass_again(k)

    @pl.when(mine)
    def _():
        many(r2.at[pl.ds(0, 15)], 2).wait_recv()

    @pl.when(jnp.logical_not(mine))
    def _():
        many(r2, 2).wait_recv()

    for k in range(1, NY):
        go(remote(r2, r3.at[x, y], x_send.at[0, k], x_recv.at[0, k], (d, t, ((y + k) % NY) * NX + x)))
    r3[x, y] = r2[...]

    for k in (3, 5):
        arrived(k)
        pass_on(k)
    for k in (2, 6):
        pass_again(k)

    @pl.when(x == y)
    def _():
        many(rr.at[core, pl.ds(0, 192)], 0).wait_recv()

    @pl.when(x != y)
    def _():
        many(rr.at[core], 0).wait_recv()

    go(remote(rr.at[core], rr.at[core], pair_send.at[3], pair_recv.at[3], (d, sibling, g)))

    arrived(4)
    pass_on(4)
    for k in range(1, NY):
        here = r3.at[x, (y + NY - k) % NY]
        remote(here, here, x_send.at[0, k], x_recv.at[0, k], (d, sibling, g)).wait_recv()
    for k in (2, 1, 3):
        go(remote(r3.at[x], r3.at[x], x_send.at[1, k], x_recv.at[1, k], (d, t, y * NX + (x + k) % NX)))
    for k in (3, 5, 4):
        pass_again(k)
    for k in (0,) + Z_ORDER:
        for tensor, sends, recvs in ((sibling, sib_send, sib_recv), ((1 - y_lo) * 2 + 1 - core, sib2_send, sib2_recv)):
            here = rows_of(tensor, k)
            remote(here, here, sends.at[k], recvs.at[k], (d, sibling, g)).wait_recv()

    for p in range(2):
        for k in (2, 1, 3):
            xs[p, k - 1] = jnp.dot(left_root[p], gbuf[p, (x + k) % NX], preferred_element_type=f32).astype(bf16)
            go(remote(xs.at[p, k - 1], xr.at[p, k - 1], x_send.at[2 + p, k], x_recv.at[2 + p, k],
                      (d, t, y * NX + (x + k) % NX)))
        ax[p] = jnp.dot(left_root[p], gbuf[p, x], preferred_element_type=f32)

    for p in range(2):
        chosen = gbuf[p, d // 2].T
        for j in range(NT):
            gr_tmp[:, j * 256 : j * 256 + 256] = jnp.dot(chosen, gbuf[p, j], preferred_element_type=f32)
        lines = gr_tmp[pl.ds((learner % 8) * 32, 32), :]
        for c in range(8):
            block = lines[:, c * 128 : c * 128 + 128]
            gs32[c, p] = block
            gs[c, p] = block.astype(bf16)

    @pl.loop(1, NG)
    def _(k):
        to = (g + k) % NG
        remote(gs.at[to // 2], gr.at[k - 1], pair_send.at[4], pair_recv.at[4], (d, t, to)).start()

    for p in range(2):
        total = ax[p]
        for k in (1, 3, 2):
            here = xr.at[p, k - 1]
            remote(here, here, x_send.at[2 + p, k], x_recv.at[2 + p, k], (d, sibling, g)).wait_recv()
            total = total + xr[p, k - 1].astype(f32)
        ax[p] = total
        for k in (2, 1, 3):
            to = (y + k) % NY
            ys[p, k - 1] = ax[p, pl.ds(to * 64, 64), :].astype(bf16)
            go(remote(ys.at[p, k - 1], yr.at[p, k - 1], x_send.at[4 + p, k], x_recv.at[4 + p, k], (d, t, to * NX + x)))

    for k in (1, 3, 2):
        here = r3.at[(x + NX - k) % NX]
        remote(here, here, x_send.at[1, k], x_recv.at[1, k], (d, sibling, g)).wait_recv()
    for a in range(NX):
        for b in range(NY):
            p, rows, c = b // 2, (b % 2) * 2 + a // 2, a % 2
            for j in range(NT):
                for z in range(4):
                    rbuf[p, j, z * 64 + rows * 16 : z * 64 + rows * 16 + 16, c * 128 : c * 128 + 128] = r3[a, b, z * NT + j]

    def left(p):
        total = None
        for j in range(NT):
            term = lax.dot_general(rbuf[p, j], gbuf[p, j], (((1,), (1,)), ((), ())), preferred_element_type=f32)
            total = term if total is None else total + term
        gram_left[p] = total

    left(0)

    many(rr.at[1 - core], 3).wait_recv()
    for p in range(2):
        total = ax[p, pl.ds(y * 64, 64), :]
        for k in (1, 3, 2):
            here = yr.at[p, k - 1]
            remote(here, here, x_send.at[4 + p, k], x_recv.at[4 + p, k], (d, sibling, g)).wait_recv()
            total = total + yr[p, k - 1].astype(f32)
        high = total.astype(bf16)
        rest = total - high.astype(f32)
        middle = rest.astype(bf16)
        low = (rest - middle.astype(f32)).astype(bf16)
        product = jnp.dot(jnp.concatenate([high, middle, low]), rr[p], preferred_element_type=f32)
        uf[p] = product[:64] + (product[64:128] + product[128:])
        for k in (2, 1, 3):
            to = (x + k) % NX
            go(remote(uf.at[p, pl.ds(to * 16, 16)], ur.at[p, k - 1], x_send.at[6 + p, k], x_recv.at[6 + p, k],
                      (d, t, y * NX + to)))

    left(1)

    many(gr, 4).wait_recv()
    for p in range(2):
        total = gs32[g // 2, p]
        for k in range(NG - 1):
            total = total + gr[k, p].astype(f32)
        gram_right[p] = jnp.where(g % 2 == 0, total[:, :64], total[:, 64:])

    for p in range(2):
        total = uf[p, pl.ds(x * 16, 16), :]
        for k in (1, 3, 2):
            here = ur.at[p, k - 1]
            remote(here, here, x_send.at[6 + p, k], x_recv.at[6 + p, k], (d, sibling, g)).wait_recv()
            total = total + ur[p, k - 1]
        update[p] = total

    for copy in sent:
        copy.wait_send()
    many(gsub.at[pl.ds(0, NG - 1)], 1).wait_send()
    many(gr, 4).wait_send()

    @pl.when(mine)
    def _():
        many(r2.at[pl.ds(0, 15)], 2).wait_send()

    @pl.when(jnp.logical_not(mine))
    def _():
        many(r2, 2).wait_send()

    @pl.when(x == y)
    def _():
        many(rr.at[core, pl.ds(0, 192)], 0).wait_send()

    @pl.when(x != y)
    def _():
        many(rr.at[core], 0).wait_send()


def shards(tokens, cotangents, left_stat, right_stat, left_root, right_root, momentum):
    vmem = pl.BlockSpec(memory_space=pltpu.VMEM)
    V, S = pltpu.VMEM, pltpu.SemaphoreType.DMA
    gram_left, gram_right, update = pl.pallas_call(
        kernel,
        out_shape=(
            jax.ShapeDtypeStruct((2, 256, 512), f32),
            jax.ShapeDtypeStruct((2, 32, 64), f32),
            jax.ShapeDtypeStruct((2, 16, 1024), f32),
        ),
        in_specs=[vmem] * 4,
        out_specs=(vmem,) * 3,
        scratch_shapes=[
            V((NZ, 2, 64, 256), f32),
            V((2, 2, 4, 64, 256), f32),
            V((2, NT, 512, 256), bf16),
            V((NG, 16, 128), bf16),
            V((NG, 16, 128), bf16),
            V((16, 16, 128), bf16),
            V((NX, NY, 16, 16, 128), bf16),
            V((2, NT, 256, 256), bf16),
            V((2, 256, 1024), bf16),
            V((2, 3, 256, 256), bf16),
            V((2, 3, 256, 256), bf16),
            V((2, 256, 256), f32),
            V((2, 3, 64, 256), bf16),
            V((2, 3, 64, 256), bf16),
            V((2, 64, 1024), f32),
            V((2, 3, 16, 1024), f32),
            V((256, 1024), f32),
            V((8, 2, 32, 128), f32),
            V((8, 2, 32, 128), bf16),
            V((NG - 1, 2, 32, 128), bf16),
            S((2, 2, 4)), S((2, 2, 4)),
            S((8,)), S((8,)),
            S((8,)), S((8,)),
            S((8,)), S((8,)),
            S((8,)), S((8,)),
            S((8, 4)), S((8, 4)),
            S((5,)), S((5,)),
        ],
        compiler_params=pltpu.CompilerParams(
            collective_id=0, has_side_effects=True, vmem_limit_bytes=48 * 1024 * 1024
        ),
    )(tokens, cotangents, left_root, right_root)
    new_left = stat_decay * left_stat + (1.0 - stat_decay) * gram_left
    new_right = stat_decay * right_stat + (1.0 - stat_decay) * gram_right
    new_momentum = momentum_decay * momentum + update
    return (new_left, new_right, new_momentum)


def solution(mesh):
    return jax.shard_map(
        shards,
        mesh=mesh,
        in_specs=(
            P("dp", "grid"),
            P(None, "dp", "tensor"),
            P(None, ("dp", "tensor"), "grid"),
            P(None, ("dp", "tensor"), "grid"),
            P(None, ("dp", "tensor"), "grid"),
            P(None, "grid", None),
            P(None, ("dp", "tensor", "grid"), None),
        ),
        out_specs=(
            P(None, ("dp", "tensor"), "grid"),
            P(None, ("dp", "tensor"), "grid"),
            P(None, ("dp", "tensor", "grid"), None),
        ),
        check_vma=False,
    )
```

```python
import jax
import jax.numpy as jnp
from jax import lax
from jax.experimental import pallas as pl
from jax.experimental.pallas import tpu as pltpu
from jax.sharding import PartitionSpec as P

MESH = pl.DeviceIdType.MESH
f32, bf16 = jnp.float32, jnp.bfloat16

stat_decay = 0.9
momentum_decay = 0.9

NZ, NT, NG, NX, NY = 8, 4, 16, 4, 4
Z_ORDER = (1, 7, 2, 6, 3, 5, 4, 8)


def remote(src, dst, send_sem, recv_sem, device):
    return pltpu.make_async_remote_copy(
        src_ref=src, dst_ref=dst, send_sem=send_sem, recv_sem=recv_sem,
        device_id=device, device_id_type=MESH,
    )


def kernel(
    tokens_hbm, cots_hbm, left_root_hbm, right_root_hbm,
    gram_left, gram_right, update,
    tokens, cots, lr, right_root,
    part, ring, gbuf, gsub, r2, r3, rbuf, rr,
    xs, xr, ax, ys, yr, uf, ur, gr_tmp, gs32, gs, gr, gl,
    ring_send, ring_recv, ag_send, ag_recv, sib_send, sib_recv, yl_send, yl_recv,
    sib2_send, sib2_recv, x_send, x_recv, pair_send, pair_recv, in_sem,
    lr_send, lr_recv, rr_send, rr_recv,
):
    d, t, g = lax.axis_index("dp"), lax.axis_index("tensor"), lax.axis_index("grid")
    y, x = g // NX, g % NX
    core, y_lo = t % 2, t // 2
    sibling = y_lo * 2 + (1 - core)
    partner = (1 - y_lo) * 2 + core
    across = (1 - y_lo) * 2 + 1 - core
    learner = d * NT + t

    loads = [
        pltpu.make_async_copy(src, dst, in_sem.at[i])
        for i, (src, dst) in enumerate(
            ((tokens_hbm, tokens), (cots_hbm, cots), (right_root_hbm, right_root), (left_root_hbm, lr.at[:, t]))
        )
    ]
    for load in loads:
        load.start()

    barrier = pltpu.get_barrier_semaphore()

    def greet(*device):
        pl.semaphore_signal(barrier, inc=1, device_id=device, device_id_type=MESH)

    rows_z, rows_t = g // 2, (g % 2) * 2 + d // 4
    mine = jnp.logical_and(rows_z == d, rows_t == t)
    source_g = 2 * d + y_lo

    @pl.loop(1, NZ)
    def _(k):
        greet((d + k) % NZ, t, g)

    greet(d, sibling, g)
    greet(d, partner, g)
    greet(d, across, g)

    @pl.loop(0, 16)
    def _(k):
        z, other = core * 4 + k // NT, k % NT

        @pl.when(jnp.logical_or(jnp.logical_or(z != d, other != t), source_g != g))
        def _():
            greet(z, other, source_g)

    @pl.loop(1, NG)
    def _(k):
        greet(d, t, (g + k) % NG)

    loads[0].wait()
    loads[1].wait()
    turned = tokens[...].T
    for p in range(2):
        whole = jnp.dot(turned, cots[p], preferred_element_type=f32)
        for z in range(NZ):
            part[z, p] = whole[z * 64 : z * 64 + 64]

    pl.semaphore_wait(barrier, NZ - 1 + 3 + NG - 1 + jnp.where(mine, 15, 16))

    loads[2].wait()

    sent = []

    def go(copy):
        copy.start()
        sent.append(copy)

    loads[3].wait()
    go(remote(lr.at[:, t], lr.at[:, t], lr_send.at[0], lr_recv.at[0], (d, partner, g)))
    go(remote(lr.at[:, t], lr.at[:, t], lr_send.at[1], lr_recv.at[1], (d, sibling, g)))

    def own_root(where):
        return rr.at[:, pl.ds(where * 64, 64), :]

    @pl.when(y == t)
    def _():
        for k in (2, 1, 3):
            remote(right_root, own_root(x), rr_send.at[k], rr_recv.at[0], (d, t, ((y + k) % NY) * NX + x)).start()
        rr[:, pl.ds(x * 64, 64), :] = right_root[...]

    up, down = ((d + 1) % NZ, t, g), ((d + NZ - 1) % NZ, t, g)

    def length(way, stream):
        return 4 if way == stream % 2 else 3

    STREAMS = ((0, 0, 0), (1, 1, 0), (2, 1, 1), (3, 0, 1))

    for step in range(4):
        for stream, p, half in STREAMS:
            rows = slice(half * 32, half * 32 + 32)
            for way in range(2):
                n = length(way, stream)
                if step >= n:
                    continue
                e = (d + n - step) % NZ if way == 0 else (d + NZ - n + step) % NZ
                if step == 0:
                    src = part.at[e, p, rows]
                else:
                    last = (way, stream, step - 1)
                    src = ring.at[last]
                    remote(src, src, ring_send.at[last], ring_recv.at[last], up).wait_recv()
                    ring[last] = ring[last] + part[e, p, rows]
                this = (way, stream, step)
                go(remote(src, ring.at[this], ring_send.at[this], ring_recv.at[this], up if way == 0 else down))
    for stream, p, half in STREAMS:
        total = part[d, p, half * 32 : half * 32 + 32]
        for way in range(2):
            last = (way, stream, length(way, stream) - 1)
            slot = ring.at[last]
            remote(slot, slot, ring_send.at[last], ring_recv.at[last], up).wait_recv()
            total = total + ring[last]
        piece = total.astype(bf16)
        gbuf[p, t, pl.ds(d * 64 + half * 32, 32), :] = piece
        for a in range(2):
            for c in range(2):
                gsub[p * 8 + (half * 2 + a) * 2 + c] = piece[a * 16 : a * 16 + 16, c * 128 : c * 128 + 128]

    def rows_of(tensor, k):
        rows = pl.ds(((d + NZ - k) % NZ) * 64, 64)
        if k in (4, 8):
            return gbuf.at[k // 4 - 1, tensor, pl.ds(((d + 4) % NZ) * 64, 64), :]
        return gbuf.at[:, tensor, rows, :]

    def along(src, k, to):
        go(remote(src, src, ag_send.at[k], ag_recv.at[k], (to % NZ, t, g)))

    along(rows_of(t, 0), 2, d + 2)
    along(rows_of(t, 0), 6, d + 6)
    along(rows_of(t, 0), 1, d + 1)
    along(rows_of(t, 0), 7, d + 7)

    def pass_on(k):
        go(remote(rows_of(t, k), rows_of(t, k), yl_send.at[k], yl_recv.at[k], (d, partner, g)))
        go(remote(rows_of(t, k), rows_of(t, k), sib_send.at[k], sib_recv.at[k], (d, sibling, g)))

    def pass_again(k):
        here = rows_of(partner, k)
        remote(here, here, yl_send.at[k], yl_recv.at[k], (d, partner, g)).wait_recv()
        go(remote(here, here, sib2_send.at[k], sib2_recv.at[k], (d, sibling, g)))

    def arrived(k):
        here = rows_of(t, k)
        remote(here, here, ag_send.at[k], ag_recv.at[k], (d, partner, g)).wait_recv()

    pass_on(0)

    def many(ref, s):
        return remote(ref, ref, pair_send.at[s], pair_recv.at[s], (d, sibling, g))

    @pl.loop(0, NG)
    def _(k):
        @pl.when(jnp.logical_or(jnp.logical_not(mine), k != g))
        def _():
            remote(gsub.at[k], r2.at[(d % 4) * NT + t], pair_send.at[1], pair_recv.at[1], (rows_z, rows_t, k)).start()

    @pl.when(mine)
    def _():
        r2[(d % 4) * NT + t] = gsub[g]

    def two_back(tensor, k, p):
        return gbuf.at[p, tensor, pl.ds(((d + NZ - k) % NZ) * 64, 64), :]

    arrived(2)
    along(two_back(t, 2, 0), 4, d + 2)
    along(rows_of(t, 2), 3, d + 1)
    arrived(6)
    along(two_back(t, 6, 1), 8, d + 6)
    along(rows_of(t, 6), 5, d + 7)
    for k in (2, 6, 1, 7):
        if k in (1, 7):
            arrived(k)
        pass_on(k)

    def lr_arrived(tensor, i):
        here = lr.at[:, tensor]
        remote(here, here, lr_send.at[i], lr_recv.at[i], (d, sibling, g)).wait_recv()

    lr_arrived(partner, 0)
    go(remote(lr.at[:, partner], lr.at[:, partner], lr_send.at[2], lr_recv.at[2], (d, sibling, g)))

    @pl.when(y != t)
    def _():
        remote(own_root(x), own_root(x), rr_send.at[0], rr_recv.at[0], (d, sibling, g)).wait_recv()

    for k in (2, 1, 3):
        go(remote(own_root(x), own_root(x), x_send.at[8, k], x_recv.at[8, k], (d, t, y * NX + (x + k) % NX)))

    @pl.when(mine)
    def _():
        many(r2.at[pl.ds(0, 15)], 1).wait_recv()

    @pl.when(jnp.logical_not(mine))
    def _():
        many(r2, 1).wait_recv()

    for k in range(1, NY):
        go(remote(r2, r3.at[x, y], x_send.at[0, k], x_recv.at[0, k], (d, t, ((y + k) % NY) * NX + x)))
    r3[x, y] = r2[...]

    lr_arrived(sibling, 1)
    lr_arrived(across, 2)
    for k in (3, 5, 4, 8):
        arrived(k)
        pass_on(k)

    def applied(p, at):
        rows = jnp.concatenate(
            [lr[p, i, pl.ds(q * 64 + at * 16, 16), :] for q in range(NY) for i in range(NT)], axis=0
        )
        return jnp.dot(rows, gbuf[p, t], preferred_element_type=f32)

    for p in range(2):
        for k in (2, 1, 3):
            xs[p, k - 1] = applied(p, (x + k) % NX).astype(bf16)
            go(remote(xs.at[p, k - 1], xr.at[p, k - 1], x_send.at[2 + p, k], x_recv.at[2 + p, k],
                      (d, t, y * NX + (x + k) % NX)))
        ax[p] = applied(p, x)

    for k in (0,) + Z_ORDER:
        pass_again(k)

    for k in range(1, NY):
        here = r3.at[x, (y + NY - k) % NY]
        remote(here, here, x_send.at[0, k], x_recv.at[0, k], (d, sibling, g)).wait_recv()
    for k in (2, 1, 3):
        go(remote(r3.at[x], r3.at[x], x_send.at[1, k], x_recv.at[1, k], (d, t, y * NX + (x + k) % NX)))

    for p in range(2):
        total = ax[p]
        for k in (1, 3, 2):
            here = xr.at[p, k - 1]
            remote(here, here, x_send.at[2 + p, k], x_recv.at[2 + p, k], (d, sibling, g)).wait_recv()
            total = total + xr[p, k - 1].astype(f32)
        ax[p] = total
        for k in (2, 1, 3):
            to = (y + k) % NY
            ys[p, k - 1] = ax[p, pl.ds(to * 64, 64), :].astype(bf16)
            go(remote(ys.at[p, k - 1], yr.at[p, k - 1], x_send.at[4 + p, k], x_recv.at[4 + p, k], (d, t, to * NX + x)))

    for k in (0,) + Z_ORDER:
        for tensor, sends, recvs in ((sibling, sib_send, sib_recv), (across, sib2_send, sib2_recv)):
            here = rows_of(tensor, k)
            remote(here, here, sends.at[k], recvs.at[k], (d, sibling, g)).wait_recv()

    for p in range(2):
        chosen = gbuf[p, d // 2].T
        for j in range(NT):
            gr_tmp[:, j * 256 : j * 256 + 256] = jnp.dot(chosen, gbuf[p, j], preferred_element_type=f32)
        lines = gr_tmp[pl.ds((learner % 8) * 32, 32), :]
        for c in range(8):
            block = lines[:, c * 128 : c * 128 + 128]
            gs32[c, p] = block
            gs[c, p] = block.astype(bf16)

    @pl.loop(1, NG)
    def _(k):
        to = (g + k) % NG
        remote(gs.at[to // 2], gr.at[k - 1], pair_send.at[4], pair_recv.at[4], (d, t, to)).start()

    def own_rows_ready():
        for k in (1, 3, 2):
            here = r3.at[(x + NX - k) % NX]
            remote(here, here, x_send.at[1, k], x_recv.at[1, k], (d, sibling, g)).wait_recv()
        for a in range(NX):
            for b in range(NY):
                p, rows, c = b // 2, (b % 2) * 2 + a // 2, a % 2
                for j in range(NT):
                    for z in range(4):
                        rbuf[p, j, z * 64 + rows * 16 : z * 64 + rows * 16 + 16, c * 128 : c * 128 + 128] = r3[a, b, z * NT + j]

    stores = [pltpu.make_async_copy(gl.at[p], gram_left.at[p], in_sem.at[4 + p]) for p in range(2)]

    def left(p):
        total = None
        for j in range(NT):
            term = lax.dot_general(rbuf[p, j], gbuf[p, j], (((1,), (1,)), ((), ())), preferred_element_type=f32)
            total = term if total is None else total + term
        gl[p] = total
        stores[p].start()

    for k in (1, 3, 2):
        here = own_root((x + NX - k) % NX)
        remote(here, here, x_send.at[8, k], x_recv.at[8, k], (d, sibling, g)).wait_recv()

    TENSOR = ((1, sibling), (2, partner), (3, across))

    for p in range(2):
        total = ax[p, pl.ds(y * 64, 64), :]
        for k in (1, 3, 2):
            here = yr.at[p, k - 1]
            remote(here, here, x_send.at[4 + p, k], x_recv.at[4 + p, k], (d, sibling, g)).wait_recv()
            total = total + yr[p, k - 1].astype(f32)
        high = total.astype(bf16)
        rest = total - high.astype(f32)
        middle = rest.astype(bf16)
        low = (rest - middle.astype(f32)).astype(bf16)
        product = jnp.dot(jnp.concatenate([high, middle, low]), rr[p], preferred_element_type=f32)
        uf[p] = product[:64] + (product[64:128] + product[128:])
        for k, to in reversed(TENSOR):
            go(remote(uf.at[p, pl.ds(to * 16, 16)], ur.at[p, k - 1], x_send.at[6 + p, k], x_recv.at[6 + p, k], (d, to, g)))

    many(gr, 4).wait_recv()
    for p in range(2):
        total = gs32[g // 2, p]
        for k in range(NG - 1):
            total = total + gr[k, p].astype(f32)
        gram_right[p] = jnp.where(g % 2 == 0, total[:, :64], total[:, 64:])

    own_rows_ready()
    left(0)
    left(1)

    for p in range(2):
        total = uf[p, pl.ds(t * 16, 16), :]
        for k in (1, 3, 2):
            here = ur.at[p, k - 1]
            remote(here, here, x_send.at[6 + p, k], x_recv.at[6 + p, k], (d, sibling, g)).wait_recv()
            total = total + ur[p, k - 1]
        update[p] = total

    for store in stores:
        store.wait()
    for copy in sent:
        copy.wait_send()
    many(gr, 4).wait_send()

    @pl.when(mine)
    def _():
        many(r2.at[pl.ds(0, 15)], 1).wait_send()

    @pl.when(jnp.logical_not(mine))
    def _():
        many(r2, 1).wait_send()

    @pl.when(y == t)
    def _():
        for k in (2, 1, 3):
            remote(right_root, own_root(x), rr_send.at[k], rr_recv.at[0], (d, sibling, g)).wait_send()


def shards(tokens, cotangents, left_stat, right_stat, left_root, right_root, momentum):
    vmem = pl.BlockSpec(memory_space=pltpu.VMEM)
    V, S = pltpu.VMEM, pltpu.SemaphoreType.DMA
    gram_left, gram_right, update = pl.pallas_call(
        kernel,
        out_shape=(
            jax.ShapeDtypeStruct((2, 256, 512), f32),
            jax.ShapeDtypeStruct((2, 32, 64), f32),
            jax.ShapeDtypeStruct((2, 16, 1024), f32),
        ),
        in_specs=[pl.BlockSpec(memory_space=pltpu.HBM)] * 4,
        out_specs=(pl.BlockSpec(memory_space=pltpu.HBM), vmem, vmem),
        scratch_shapes=[
            V(tokens.shape, bf16),
            V(cotangents.shape, bf16),
            V((2, NT, 256, 512), bf16),
            V(right_root.shape, bf16),
            V((NZ, 2, 64, 256), f32),
            V((2, 4, 4, 32, 256), f32),
            V((2, NT, 512, 256), bf16),
            V((NG, 16, 128), bf16),
            V((16, 16, 128), bf16),
            V((NX, NY, 16, 16, 128), bf16),
            V((2, NT, 256, 256), bf16),
            V((2, 256, 1024), bf16),
            V((2, 3, 256, 256), bf16),
            V((2, 3, 256, 256), bf16),
            V((2, 256, 256), f32),
            V((2, 3, 64, 256), bf16),
            V((2, 3, 64, 256), bf16),
            V((2, 64, 1024), f32),
            V((2, 3, 16, 1024), f32),
            V((256, 1024), f32),
            V((8, 2, 32, 128), f32),
            V((8, 2, 32, 128), bf16),
            V((NG - 1, 2, 32, 128), bf16),
            V((2, 256, 512), f32),
            S((2, 4, 4)), S((2, 4, 4)),
            S((9,)), S((9,)),
            S((9,)), S((9,)),
            S((9,)), S((9,)),
            S((9,)), S((9,)),
            S((9, 4)), S((9, 4)),
            S((5,)), S((5,)),
            S((6,)),
            S((3,)), S((3,)),
            S((4,)), S((1,)),
        ],
        compiler_params=pltpu.CompilerParams(
            collective_id=0, has_side_effects=True, vmem_limit_bytes=60 * 1024 * 1024
        ),
    )(tokens, cotangents, left_root, right_root)
    new_left = stat_decay * left_stat + (1.0 - stat_decay) * gram_left
    new_right = stat_decay * right_stat + (1.0 - stat_decay) * gram_right
    new_momentum = momentum_decay * momentum + update
    return (new_left, new_right, new_momentum)


def solution(mesh):
    return jax.shard_map(
        shards,
        mesh=mesh,
        in_specs=(
            P("dp", "grid"),
            P(None, "dp", "tensor"),
            P(None, ("dp", "tensor"), "grid"),
            P(None, ("dp", "tensor"), "grid"),
            P(None, ("dp", "tensor"), "grid"),
            P(None, "grid", None),
            P(None, ("dp", "tensor", "grid"), None),
        ),
        out_specs=(
            P(None, ("dp", "tensor"), "grid"),
            P(None, ("dp", "tensor"), "grid"),
            P(None, ("dp", "tensor", "grid"), None),
        ),
        check_vma=False,
    )
```

```python
import jax
import jax.numpy as jnp
from jax import lax
from jax.experimental import pallas as pl
from jax.experimental.pallas import tpu as pltpu
from jax.sharding import PartitionSpec as P

MESH = pl.DeviceIdType.MESH
f32, bf16 = jnp.float32, jnp.bfloat16

stat_decay = 0.9
momentum_decay = 0.9

NZ, NT, NG, NX, NY = 8, 4, 16, 4, 4
Z_ORDER = (2, 6, 1, 7, 3, 5, 4)


def remote(src, dst, send_sem, recv_sem, device):
    return pltpu.make_async_remote_copy(
        src_ref=src, dst_ref=dst, send_sem=send_sem, recv_sem=recv_sem,
        device_id=device, device_id_type=MESH,
    )


def kernel(
    tokens_hbm, cots_hbm, left_root_hbm, right_root_hbm,
    gram_left, gram_right, update,
    tokens, cots, lr, right_root,
    part, ring, gbuf, gsub, r2, r3, rbuf, rr,
    xs, xr, ax, ys, yr, uf, ur, gr_tmp, gs32, gs, gr, gl,
    ring_send, ring_recv, ag_send, ag_recv, sib_send, sib_recv, yl_send, yl_recv,
    sib2_send, sib2_recv, x_send, x_recv, pair_send, pair_recv, in_sem,
    lr_send, lr_recv, rr_send, rr_recv,
):
    d, t, g = lax.axis_index("dp"), lax.axis_index("tensor"), lax.axis_index("grid")
    y, x = g // NX, g % NX
    core, y_lo = t % 2, t // 2
    sibling = y_lo * 2 + (1 - core)
    partner = (1 - y_lo) * 2 + core
    across = (1 - y_lo) * 2 + 1 - core
    learner = d * NT + t

    loads = [
        pltpu.make_async_copy(src, dst, in_sem.at[i])
        for i, (src, dst) in enumerate(
            ((tokens_hbm, tokens), (cots_hbm, cots), (right_root_hbm, right_root), (left_root_hbm, lr.at[:, t]))
        )
    ]
    for load in loads:
        load.start()

    barrier = pltpu.get_barrier_semaphore()

    def greet(*device):
        pl.semaphore_signal(barrier, inc=1, device_id=device, device_id_type=MESH)

    rows_z, rows_t = g // 2, (g % 2) * 2 + d // 4
    mine = jnp.logical_and(rows_z == d, rows_t == t)
    source_g = 2 * d + y_lo

    @pl.loop(1, NZ)
    def _(k):
        greet((d + k) % NZ, t, g)

    greet(d, sibling, g)
    greet(d, partner, g)
    greet(d, across, g)

    @pl.loop(0, 16)
    def _(k):
        z, other = core * 4 + k // NT, k % NT

        @pl.when(jnp.logical_or(jnp.logical_or(z != d, other != t), source_g != g))
        def _():
            greet(z, other, source_g)

    @pl.loop(1, NG)
    def _(k):
        greet(d, t, (g + k) % NG)

    loads[0].wait()
    loads[1].wait()
    turned = tokens[...].T
    for p in range(2):
        whole = jnp.dot(turned, cots[p], preferred_element_type=f32)
        for z in range(NZ):
            part[z, p] = whole[z * 64 : z * 64 + 64]

    pl.semaphore_wait(barrier, NZ - 1 + 3 + NG - 1 + jnp.where(mine, 15, 16))

    loads[2].wait()

    sent = []

    def go(copy):
        copy.start()
        sent.append(copy)

    def own_root(where):
        return rr.at[:, pl.ds(where * 64, 64), :]

    @pl.when(y == t)
    def _():
        for k in (2, 1, 3):
            remote(right_root, own_root(x), rr_send.at[k], rr_recv.at[0], (d, t, ((y + k) % NY) * NX + x)).start()
        rr[:, pl.ds(x * 64, 64), :] = right_root[...]

    up, down = ((d + 1) % NZ, t, g), ((d + NZ - 1) % NZ, t, g)

    def length(way, stream):
        return 4 if way == stream % 2 else 3

    STREAMS = ((0, 0, 0), (1, 1, 0), (2, 1, 1), (3, 0, 1))

    for step in range(4):
        for stream, p, half in STREAMS:
            rows = slice(half * 32, half * 32 + 32)
            for way in range(2):
                n = length(way, stream)
                if step >= n:
                    continue
                e = (d + n - step) % NZ if way == 0 else (d + NZ - n + step) % NZ
                if step == 0:
                    src = part.at[e, p, rows]
                else:
                    last = (way, stream, step - 1)
                    src = ring.at[last]
                    remote(src, src, ring_send.at[last], ring_recv.at[last], up).wait_recv()
                    ring[last] = ring[last] + part[e, p, rows]
                this = (way, stream, step)
                go(remote(src, ring.at[this], ring_send.at[this], ring_recv.at[this], up if way == 0 else down))
        if step == 1:
            loads[3].wait()
            go(remote(lr.at[:, t], lr.at[:, t], lr_send.at[0], lr_recv.at[0], (d, partner, g)))
            go(remote(lr.at[:, t], lr.at[:, t], lr_send.at[1], lr_recv.at[1], (d, sibling, g)))

    def rows_of(tensor, k):
        return gbuf.at[:, tensor, pl.ds(((d + NZ - k) % NZ) * 64, 64), :]

    def half_of(p, tensor, k):
        return gbuf.at[p, tensor, pl.ds(((d + NZ - k) % NZ) * 64, 64), :]

    def along(p, k, to, arrives):
        here = half_of(p, t, k)
        go(remote(here, here, ag_send.at[p, arrives], ag_recv.at[p, arrives], (to % NZ, t, g)))

    def arrived(p, k):
        here = half_of(p, t, k)
        remote(here, here, ag_send.at[p, k], ag_recv.at[p, k], (d, partner, g)).wait_recv()

    for q in range(2):
        for stream, p, half in STREAMS:
            if p != q:
                continue
            total = part[d, p, half * 32 : half * 32 + 32]
            for way in range(2):
                last = (way, stream, length(way, stream) - 1)
                slot = ring.at[last]
                remote(slot, slot, ring_send.at[last], ring_recv.at[last], up).wait_recv()
                total = total + ring[last]
            piece = total.astype(bf16)
            gbuf[p, t, pl.ds(d * 64 + half * 32, 32), :] = piece
            for a in range(2):
                for c in range(2):
                    gsub[p * 8 + (half * 2 + a) * 2 + c] = piece[a * 16 : a * 16 + 16, c * 128 : c * 128 + 128]
        along(q, 0, d + 2, 2)
        along(q, 0, d + 6, 6)
        along(q, 0, d + 1, 1)
        along(q, 0, d + 7, 7)

    def pass_on(k):
        go(remote(rows_of(t, k), rows_of(t, k), yl_send.at[k], yl_recv.at[k], (d, partner, g)))
        go(remote(rows_of(t, k), rows_of(t, k), sib_send.at[k], sib_recv.at[k], (d, sibling, g)))

    def pass_again(k):
        here = rows_of(partner, k)
        remote(here, here, yl_send.at[k], yl_recv.at[k], (d, partner, g)).wait_recv()
        go(remote(here, here, sib2_send.at[k], sib2_recv.at[k], (d, sibling, g)))

    def many(ref, s):
        return remote(ref, ref, pair_send.at[s], pair_recv.at[s], (d, sibling, g))

    @pl.loop(0, NG)
    def _(k):
        @pl.when(jnp.logical_or(jnp.logical_not(mine), k != g))
        def _():
            remote(gsub.at[k], r2.at[(d % 4) * NT + t], pair_send.at[1], pair_recv.at[1], (rows_z, rows_t, k)).start()

    @pl.when(mine)
    def _():
        r2[(d % 4) * NT + t] = gsub[g]

    pass_on(0)

    for p in range(2):
        arrived(p, 2)
        if p == 0:
            along(p, 2, d + 2, 4)
        along(p, 2, d + 1, 3)
        arrived(p, 6)
        if p == 1:
            along(p, 6, d + 6, 4)
        along(p, 6, d + 7, 5)

    def lr_arrived(tensor, i):
        here = lr.at[:, tensor]
        remote(here, here, lr_send.at[i], lr_recv.at[i], (d, sibling, g)).wait_recv()

    def next_x(k):
        return (d, t, y * NX + (x + k) % NX)

    def spread_x(here, row):
        for k in (1, 3):
            go(remote(here(x), here(x), x_send.at[row, k], x_recv.at[row, k], next_x(k)))

    def spread_on(here, part_of, row):
        for k in (1, 3):
            at = (x + NX - k) % NX
            remote(here(at), here(at), x_send.at[row, k], x_recv.at[row, k], (d, sibling, g)).wait_recv()
            half = part_of(k // 2, at)
            go(remote(half, half, x_send.at[row, k - 1], x_recv.at[row, k - 1], next_x(k)))

    def spread_done(part_of, row):
        for k in (1, 3):
            half = part_of(k // 2, (x + 2) % NX)
            remote(half, half, x_send.at[row, k - 1], x_recv.at[row, k - 1], (d, sibling, g)).wait_recv()

    def root_half(p, where):
        return rr.at[p, pl.ds(where * 64, 64), :]

    @pl.when(y != t)
    def _():
        remote(own_root(x), own_root(x), rr_send.at[0], rr_recv.at[0], (d, sibling, g)).wait_recv()

    spread_x(own_root, 8)
    lr_arrived(partner, 0)
    go(remote(lr.at[:, partner], lr.at[:, partner], lr_send.at[2], lr_recv.at[2], (d, sibling, g)))

    @pl.when(mine)
    def _():
        many(r2.at[pl.ds(0, 15)], 1).wait_recv()

    @pl.when(jnp.logical_not(mine))
    def _():
        many(r2, 1).wait_recv()

    for k in range(1, NY):
        go(remote(r2, r3.at[x, y], x_send.at[0, k], x_recv.at[0, k], (d, t, ((y + k) % NY) * NX + x)))
    r3[x, y] = r2[...]

    lr_arrived(sibling, 1)
    lr_arrived(across, 2)

    def applied(p, at):
        rows = jnp.concatenate(
            [lr[p, i, pl.ds(q * 64 + at * 16, 16), :] for q in range(NY) for i in range(NT)], axis=0
        )
        return jnp.dot(rows, gbuf[p, t], preferred_element_type=f32)

    for p in range(2):
        for k in (1, 7, 3, 5, 4):
            arrived(p, k)
        for k in (2, 1, 3):
            xs[p, k - 1] = applied(p, (x + k) % NX).astype(bf16)
            go(remote(xs.at[p, k - 1], xr.at[p, k - 1], x_send.at[2 + p, k], x_recv.at[2 + p, k], next_x(k)))
        ax[p] = applied(p, x)

    for k in Z_ORDER:
        pass_on(k)
    spread_on(own_root, root_half, 8)

    def rows_at(where):
        return r3.at[where]

    def rows_half(half, where):
        return r3.at[where, half * 2 : half * 2 + 2]

    def sum_x(p):
        total = ax[p]
        for k in (1, 3, 2):
            here = xr.at[p, k - 1]
            remote(here, here, x_send.at[2 + p, k], x_recv.at[2 + p, k], (d, sibling, g)).wait_recv()
            total = total + xr[p, k - 1].astype(f32)
        ax[p] = total
        for k in (2, 1, 3):
            to = (y + k) % NY
            ys[p, k - 1] = ax[p, pl.ds(to * 64, 64), :].astype(bf16)
            go(remote(ys.at[p, k - 1], yr.at[p, k - 1], x_send.at[4 + p, k], x_recv.at[4 + p, k], (d, t, to * NX + x)))

    sum_x(0)
    for k in range(1, NY):
        here = r3.at[x, (y + NY - k) % NY]
        remote(here, here, x_send.at[0, k], x_recv.at[0, k], (d, sibling, g)).wait_recv()
    spread_x(rows_at, 1)
    sum_x(1)

    def own_rows_ready():
        spread_done(rows_half, 1)
        for a in range(NX):
            for b in range(NY):
                p, rows, c = b // 2, (b % 2) * 2 + a // 2, a % 2
                for j in range(NT):
                    for z in range(4):
                        rbuf[p, j, z * 64 + rows * 16 : z * 64 + rows * 16 + 16, c * 128 : c * 128 + 128] = r3[a, b, z * NT + j]

    stores = [pltpu.make_async_copy(gl.at[p], gram_left.at[p], in_sem.at[4 + p]) for p in range(2)]

    def left(p):
        total = None
        for j in range(NT):
            term = lax.dot_general(rbuf[p, j], gbuf[p, j], (((1,), (1,)), ((), ())), preferred_element_type=f32)
            total = term if total is None else total + term
        gl[p] = total
        stores[p].start()

    spread_done(root_half, 8)

    TENSOR = ((1, sibling), (2, partner), (3, across))

    def finish(p):
        total = ax[p, pl.ds(y * 64, 64), :]
        for k in (1, 3, 2):
            here = yr.at[p, k - 1]
            remote(here, here, x_send.at[4 + p, k], x_recv.at[4 + p, k], (d, sibling, g)).wait_recv()
            total = total + yr[p, k - 1].astype(f32)
        high = total.astype(bf16)
        rest = total - high.astype(f32)
        middle = rest.astype(bf16)
        low = (rest - middle.astype(f32)).astype(bf16)
        product = jnp.dot(jnp.concatenate([high, middle, low]), rr[p], preferred_element_type=f32)
        uf[p] = product[:64] + (product[64:128] + product[128:])
        for k, to in reversed(TENSOR):
            go(remote(uf.at[p, pl.ds(to * 16, 16)], ur.at[p, k - 1], x_send.at[6 + p, k], x_recv.at[6 + p, k], (d, to, g)))

    finish(0)
    spread_on(rows_at, rows_half, 1)
    for k in (0,) + Z_ORDER:
        pass_again(k)
    for k in (0,) + Z_ORDER:
        for tensor, sends, recvs in ((sibling, sib_send, sib_recv), (across, sib2_send, sib2_recv)):
            here = rows_of(tensor, k)
            remote(here, here, sends.at[k], recvs.at[k], (d, sibling, g)).wait_recv()

    for p in range(2):
        chosen = gbuf[p, d // 2].T
        for j in range(NT):
            gr_tmp[:, j * 256 : j * 256 + 256] = jnp.dot(chosen, gbuf[p, j], preferred_element_type=f32)
        lines = gr_tmp[pl.ds((learner % 8) * 32, 32), :]
        for c in range(8):
            block = lines[:, c * 128 : c * 128 + 128]
            gs32[c, p] = block
            gs[c, p] = block.astype(bf16)

    @pl.loop(1, NG)
    def _(k):
        to = (g + k) % NG
        remote(gs.at[to // 2], gr.at[k - 1], pair_send.at[4], pair_recv.at[4], (d, t, to)).start()

    finish(1)

    own_rows_ready()
    left(0)
    left(1)

    many(gr, 4).wait_recv()
    for p in range(2):
        total = gs32[g // 2, p]
        for k in range(NG - 1):
            total = total + gr[k, p].astype(f32)
        gram_right[p] = jnp.where(g % 2 == 0, total[:, :64], total[:, 64:])

    for p in range(2):
        total = uf[p, pl.ds(t * 16, 16), :]
        for k in (1, 3, 2):
            here = ur.at[p, k - 1]
            remote(here, here, x_send.at[6 + p, k], x_recv.at[6 + p, k], (d, sibling, g)).wait_recv()
            total = total + ur[p, k - 1]
        update[p] = total

    for store in stores:
        store.wait()
    for copy in sent:
        copy.wait_send()
    many(gr, 4).wait_send()

    @pl.when(mine)
    def _():
        many(r2.at[pl.ds(0, 15)], 1).wait_send()

    @pl.when(jnp.logical_not(mine))
    def _():
        many(r2, 1).wait_send()

    @pl.when(y == t)
    def _():
        for k in (2, 1, 3):
            remote(right_root, own_root(x), rr_send.at[k], rr_recv.at[0], (d, sibling, g)).wait_send()


def outputs(left_stat, gram_left, right_stat, gram_right, momentum, update, new_left, new_right, new_momentum):
    new_left[...] = stat_decay * left_stat[...] + (1.0 - stat_decay) * gram_left[...]
    new_right[...] = stat_decay * right_stat[...] + (1.0 - stat_decay) * gram_right[...]
    new_momentum[...] = momentum_decay * momentum[...] + update[...]


def shards(tokens, cotangents, left_stat, right_stat, left_root, right_root, momentum):
    vmem = pl.BlockSpec(memory_space=pltpu.VMEM)
    V, S = pltpu.VMEM, pltpu.SemaphoreType.DMA
    gram_left, gram_right, update = pl.pallas_call(
        kernel,
        out_shape=(
            jax.ShapeDtypeStruct((2, 256, 512), f32),
            jax.ShapeDtypeStruct((2, 32, 64), f32),
            jax.ShapeDtypeStruct((2, 16, 1024), f32),
        ),
        in_specs=[pl.BlockSpec(memory_space=pltpu.HBM)] * 4,
        out_specs=(pl.BlockSpec(memory_space=pltpu.HBM), vmem, vmem),
        scratch_shapes=[
            V(tokens.shape, bf16),
            V(cotangents.shape, bf16),
            V((2, NT, 256, 512), bf16),
            V(right_root.shape, bf16),
            V((NZ, 2, 64, 256), f32),
            V((2, 4, 4, 32, 256), f32),
            V((2, NT, 512, 256), bf16),
            V((NG, 16, 128), bf16),
            V((16, 16, 128), bf16),
            V((NX, NY, 16, 16, 128), bf16),
            V((2, NT, 256, 256), bf16),
            V((2, 256, 1024), bf16),
            V((2, 3, 256, 256), bf16),
            V((2, 3, 256, 256), bf16),
            V((2, 256, 256), f32),
            V((2, 3, 64, 256), bf16),
            V((2, 3, 64, 256), bf16),
            V((2, 64, 1024), f32),
            V((2, 3, 16, 1024), f32),
            V((256, 1024), f32),
            V((8, 2, 32, 128), f32),
            V((8, 2, 32, 128), bf16),
            V((NG - 1, 2, 32, 128), bf16),
            V((2, 256, 512), f32),
            S((2, 4, 4)), S((2, 4, 4)),
            S((2, 8)), S((2, 8)),
            S((8,)), S((8,)),
            S((8,)), S((8,)),
            S((8,)), S((8,)),
            S((9, 4)), S((9, 4)),
            S((5,)), S((5,)),
            S((6,)),
            S((3,)), S((3,)),
            S((4,)), S((1,)),
        ],
        compiler_params=pltpu.CompilerParams(
            collective_id=0, has_side_effects=True, vmem_limit_bytes=60 * 1024 * 1024
        ),
    )(tokens, cotangents, left_root, right_root)
    arrays = (left_stat, gram_left, right_stat, gram_right, momentum, update)
    blocks = [pl.BlockSpec((1, *array.shape[1:]), lambda p: (p, 0, 0)) for array in arrays]
    return pl.pallas_call(
        outputs,
        grid=(2,),
        out_shape=tuple(jax.ShapeDtypeStruct(array.shape, f32) for array in arrays[::2]),
        in_specs=blocks,
        out_specs=tuple(blocks[::2]),
        name="outputs",
    )(*arrays)


def solution(mesh):
    return jax.shard_map(
        shards,
        mesh=mesh,
        in_specs=(
            P("dp", "grid"),
            P(None, "dp", "tensor"),
            P(None, ("dp", "tensor"), "grid"),
            P(None, ("dp", "tensor"), "grid"),
            P(None, ("dp", "tensor"), "grid"),
            P(None, "grid", None),
            P(None, ("dp", "tensor", "grid"), None),
        ),
        out_specs=(
            P(None, ("dp", "tensor"), "grid"),
            P(None, ("dp", "tensor"), "grid"),
            P(None, ("dp", "tensor", "grid"), None),
        ),
        check_vma=False,
    )
```

```python
import jax
import jax.numpy as jnp
from jax import lax
from jax.experimental import pallas as pl
from jax.experimental.pallas import tpu as pltpu
from jax.sharding import PartitionSpec as P

MESH = pl.DeviceIdType.MESH
f32, bf16 = jnp.float32, jnp.bfloat16

stat_decay = 0.9
momentum_decay = 0.9

NZ, NT, NG, NX, NY = 8, 4, 16, 4, 4
Z_ORDER = (2, 6, 1, 7, 3, 5, 4)


def remote(src, dst, send_sem, recv_sem, device):
    return pltpu.make_async_remote_copy(
        src_ref=src, dst_ref=dst, send_sem=send_sem, recv_sem=recv_sem,
        device_id=device, device_id_type=MESH,
    )


def kernel(
    tokens_hbm, cots_hbm, left_root_hbm, right_root_hbm,
    gram_left, gram_right, update,
    tokens, cots, lr, right_root,
    part, ring, gbuf, gsub, r2, r3, rbuf, rr,
    xs, xr, ax, ys, yr, uf, ur, gr_tmp, gs32, gs, gr, gl,
    ring_send, ring_recv, ag_send, ag_recv, sib_send, sib_recv, yl_send, yl_recv,
    sib2_send, sib2_recv, x_send, x_recv, pair_send, pair_recv, in_sem,
    lr_send, lr_recv, rr_send, rr_recv,
):
    d, t, g = lax.axis_index("dp"), lax.axis_index("tensor"), lax.axis_index("grid")
    y, x = g // NX, g % NX
    core, y_lo = t % 2, t // 2
    sibling = y_lo * 2 + (1 - core)
    partner = (1 - y_lo) * 2 + core
    across = (1 - y_lo) * 2 + 1 - core
    learner = d * NT + t

    loads = [
        pltpu.make_async_copy(src, dst, in_sem.at[i])
        for i, (src, dst) in enumerate(
            ((tokens_hbm, tokens), (cots_hbm, cots), (right_root_hbm, right_root), (left_root_hbm, lr.at[:, t]))
        )
    ]
    for load in loads:
        load.start()

    barrier = pltpu.get_barrier_semaphore()

    def greet(*device):
        pl.semaphore_signal(barrier, inc=1, device_id=device, device_id_type=MESH)

    rows_z, rows_t = g // 2, (g % 2) * 2 + d // 4
    mine = jnp.logical_and(rows_z == d, rows_t == t)
    source_g = 2 * d + y_lo

    @pl.loop(1, NZ)
    def _(k):
        greet((d + k) % NZ, t, g)

    greet(d, sibling, g)
    greet(d, partner, g)
    greet(d, across, g)

    @pl.loop(0, 16)
    def _(k):
        z, other = core * 4 + k // NT, k % NT

        @pl.when(jnp.logical_or(jnp.logical_or(z != d, other != t), source_g != g))
        def _():
            greet(z, other, source_g)

    @pl.loop(1, NG)
    def _(k):
        greet(d, t, (g + k) % NG)

    loads[0].wait()
    loads[1].wait()
    turned = tokens[...].T
    for p in range(2):
        whole = jnp.dot(turned, cots[p], preferred_element_type=f32)
        for z in range(NZ):
            part[z, p] = whole[z * 64 : z * 64 + 64]

    pl.semaphore_wait(barrier, NZ - 1 + 3 + NG - 1 + jnp.where(mine, 15, 16))

    loads[2].wait()

    sent = []

    def go(copy):
        copy.start()
        sent.append(copy)

    def own_root(where):
        return rr.at[:, pl.ds(where * 64, 64), :]

    @pl.when(y == t)
    def _():
        for k in (2, 1, 3):
            remote(right_root, own_root(x), rr_send.at[k], rr_recv.at[0], (d, t, ((y + k) % NY) * NX + x)).start()
        rr[:, pl.ds(x * 64, 64), :] = right_root[...]

    up, down = ((d + 1) % NZ, t, g), ((d + NZ - 1) % NZ, t, g)

    def length(way, stream):
        return 4 if way == stream % 2 else 3

    STREAMS = ((0, 0, 0), (1, 1, 0), (2, 1, 1), (3, 0, 1))

    for step in range(4):
        for stream, p, half in STREAMS:
            rows = slice(half * 32, half * 32 + 32)
            for way in range(2):
                n = length(way, stream)
                if step >= n:
                    continue
                e = (d + n - step) % NZ if way == 0 else (d + NZ - n + step) % NZ
                if step == 0:
                    src = part.at[e, p, rows]
                else:
                    last = (way, stream, step - 1)
                    src = ring.at[last]
                    remote(src, src, ring_send.at[last], ring_recv.at[last], up).wait_recv()
                    ring[last] = ring[last] + part[e, p, rows]
                this = (way, stream, step)
                go(remote(src, ring.at[this], ring_send.at[this], ring_recv.at[this], up if way == 0 else down))
        if step == 1:
            loads[3].wait()
            go(remote(lr.at[:, t], lr.at[:, t], lr_send.at[0], lr_recv.at[0], (d, partner, g)))
            go(remote(lr.at[:, t], lr.at[:, t], lr_send.at[1], lr_recv.at[1], (d, sibling, g)))

    def rows_of(tensor, k):
        return gbuf.at[:, tensor, pl.ds(((d + NZ - k) % NZ) * 64, 64), :]

    def half_of(p, tensor, k):
        return gbuf.at[p, tensor, pl.ds(((d + NZ - k) % NZ) * 64, 64), :]

    def along(p, k, to, arrives):
        here = half_of(p, t, k)
        go(remote(here, here, ag_send.at[p, arrives], ag_recv.at[p, arrives], (to % NZ, t, g)))

    def arrived(p, k):
        here = half_of(p, t, k)
        remote(here, here, ag_send.at[p, k], ag_recv.at[p, k], (d, partner, g)).wait_recv()

    for q in range(2):
        for stream, p, half in STREAMS:
            if p != q:
                continue
            total = part[d, p, half * 32 : half * 32 + 32]
            for way in range(2):
                last = (way, stream, length(way, stream) - 1)
                slot = ring.at[last]
                remote(slot, slot, ring_send.at[last], ring_recv.at[last], up).wait_recv()
                total = total + ring[last]
            piece = total.astype(bf16)
            gbuf[p, t, pl.ds(d * 64 + half * 32, 32), :] = piece
            for a in range(2):
                for c in range(2):
                    gsub[p * 8 + (half * 2 + a) * 2 + c] = piece[a * 16 : a * 16 + 16, c * 128 : c * 128 + 128]
        along(q, 0, d + 2, 2)
        along(q, 0, d + 6, 6)
        along(q, 0, d + 1, 1)
        along(q, 0, d + 7, 7)

    def pass_on(k):
        go(remote(rows_of(t, k), rows_of(t, k), yl_send.at[k], yl_recv.at[k], (d, partner, g)))
        go(remote(rows_of(t, k), rows_of(t, k), sib_send.at[k], sib_recv.at[k], (d, sibling, g)))

    def pass_again(k):
        here = rows_of(partner, k)
        remote(here, here, yl_send.at[k], yl_recv.at[k], (d, partner, g)).wait_recv()
        go(remote(here, here, sib2_send.at[k], sib2_recv.at[k], (d, sibling, g)))

    def many(ref, s):
        return remote(ref, ref, pair_send.at[s], pair_recv.at[s], (d, sibling, g))

    @pl.loop(0, NG)
    def _(k):
        @pl.when(jnp.logical_or(jnp.logical_not(mine), k != g))
        def _():
            remote(gsub.at[k], r2.at[(d % 4) * NT + t], pair_send.at[1], pair_recv.at[1], (rows_z, rows_t, k)).start()

    @pl.when(mine)
    def _():
        r2[(d % 4) * NT + t] = gsub[g]

    pass_on(0)

    def next_x(k):
        return (d, t, y * NX + (x + k) % NX)

    def spread_x(here, row):
        for k in (1, 3):
            go(remote(here(x), here(x), x_send.at[row, k], x_recv.at[row, k], next_x(k)))

    def spread_on(here, part_of, row):
        for k in (1, 3):
            at = (x + NX - k) % NX
            remote(here(at), here(at), x_send.at[row, k], x_recv.at[row, k], (d, sibling, g)).wait_recv()
            half = part_of(k // 2, at)
            go(remote(half, half, x_send.at[row, k - 1], x_recv.at[row, k - 1], next_x(k)))

    def spread_done(part_of, row):
        for k in (1, 3):
            half = part_of(k // 2, (x + 2) % NX)
            remote(half, half, x_send.at[row, k - 1], x_recv.at[row, k - 1], (d, sibling, g)).wait_recv()

    def root_half(p, where):
        return rr.at[p, pl.ds(where * 64, 64), :]

    @pl.when(y != t)
    def _():
        remote(own_root(x), own_root(x), rr_send.at[0], rr_recv.at[0], (d, sibling, g)).wait_recv()

    spread_x(own_root, 8)

    for p in range(2):
        arrived(p, 2)
        if p == 0:
            along(p, 2, d + 2, 4)
        along(p, 2, d + 1, 3)
        arrived(p, 6)
        if p == 1:
            along(p, 6, d + 6, 4)
        along(p, 6, d + 7, 5)

    for k in (2, 6):
        pass_on(k)

    def lr_arrived(tensor, i):
        here = lr.at[:, tensor]
        remote(here, here, lr_send.at[i], lr_recv.at[i], (d, sibling, g)).wait_recv()

    lr_arrived(partner, 0)
    go(remote(lr.at[:, partner], lr.at[:, partner], lr_send.at[2], lr_recv.at[2], (d, sibling, g)))

    @pl.when(mine)
    def _():
        many(r2.at[pl.ds(0, 15)], 1).wait_recv()

    @pl.when(jnp.logical_not(mine))
    def _():
        many(r2, 1).wait_recv()

    for k in range(1, NY):
        go(remote(r2, r3.at[x, y], x_send.at[0, k], x_recv.at[0, k], (d, t, ((y + k) % NY) * NX + x)))
    r3[x, y] = r2[...]

    lr_arrived(sibling, 1)
    lr_arrived(across, 2)

    def applied(p, at):
        rows = jnp.concatenate(
            [lr[p, i, pl.ds(q * 64 + at * 16, 16), :] for q in range(NY) for i in range(NT)], axis=0
        )
        return jnp.dot(rows, gbuf[p, t], preferred_element_type=f32)

    for p in range(2):
        for k in (1, 7, 3, 5, 4):
            arrived(p, k)
        for k in (2, 1, 3):
            xs[p, k - 1] = applied(p, (x + k) % NX).astype(bf16)
            go(remote(xs.at[p, k - 1], xr.at[p, k - 1], x_send.at[2 + p, k], x_recv.at[2 + p, k], next_x(k)))
        ax[p] = applied(p, x)

    for k in Z_ORDER[2:]:
        pass_on(k)
    spread_on(own_root, root_half, 8)

    def rows_at(where):
        return r3.at[where]

    def rows_half(half, where):
        return r3.at[where, half * 2 : half * 2 + 2]

    def sum_x(p):
        total = ax[p]
        for k in (1, 3, 2):
            here = xr.at[p, k - 1]
            remote(here, here, x_send.at[2 + p, k], x_recv.at[2 + p, k], (d, sibling, g)).wait_recv()
            total = total + xr[p, k - 1].astype(f32)
        ax[p] = total
        for k in (2, 1, 3):
            to = (y + k) % NY
            ys[p, k - 1] = ax[p, pl.ds(to * 64, 64), :].astype(bf16)
            go(remote(ys.at[p, k - 1], yr.at[p, k - 1], x_send.at[4 + p, k], x_recv.at[4 + p, k], (d, t, to * NX + x)))

    sum_x(0)
    for k in range(1, NY):
        here = r3.at[x, (y + NY - k) % NY]
        remote(here, here, x_send.at[0, k], x_recv.at[0, k], (d, sibling, g)).wait_recv()
    spread_x(rows_at, 1)
    for k in (0,) + Z_ORDER:
        pass_again(k)
    sum_x(1)

    def own_rows_ready():
        spread_done(rows_half, 1)
        for a in range(NX):
            for b in range(NY):
                p, rows, c = b // 2, (b % 2) * 2 + a // 2, a % 2
                for j in range(NT):
                    for z in range(4):
                        rbuf[p, j, z * 64 + rows * 16 : z * 64 + rows * 16 + 16, c * 128 : c * 128 + 128] = r3[a, b, z * NT + j]

    stores = [pltpu.make_async_copy(gl.at[p], gram_left.at[p], in_sem.at[4 + p]) for p in range(2)]

    def left(p):
        total = None
        for j in range(NT):
            term = lax.dot_general(rbuf[p, j], gbuf[p, j], (((1,), (1,)), ((), ())), preferred_element_type=f32)
            total = term if total is None else total + term
        gl[p] = total
        stores[p].start()

    spread_done(root_half, 8)

    TENSOR = ((1, sibling), (2, partner), (3, across))

    def finish(p):
        total = ax[p, pl.ds(y * 64, 64), :]
        for k in (1, 3, 2):
            here = yr.at[p, k - 1]
            remote(here, here, x_send.at[4 + p, k], x_recv.at[4 + p, k], (d, sibling, g)).wait_recv()
            total = total + yr[p, k - 1].astype(f32)
        high = total.astype(bf16)
        rest = total - high.astype(f32)
        middle = rest.astype(bf16)
        low = (rest - middle.astype(f32)).astype(bf16)
        product = jnp.dot(jnp.concatenate([high, middle, low]), rr[p], preferred_element_type=f32)
        uf[p] = product[:64] + (product[64:128] + product[128:])
        for k, to in reversed(TENSOR):
            go(remote(uf.at[p, pl.ds(to * 16, 16)], ur.at[p, k - 1], x_send.at[6 + p, k], x_recv.at[6 + p, k], (d, to, g)))

    for k in (0,) + Z_ORDER:
        for tensor, sends, recvs in ((sibling, sib_send, sib_recv), (across, sib2_send, sib2_recv)):
            here = rows_of(tensor, k)
            remote(here, here, sends.at[k], recvs.at[k], (d, sibling, g)).wait_recv()

    for p in range(2):
        chosen = gbuf[p, d // 2].T
        for j in range(NT):
            gr_tmp[:, j * 256 : j * 256 + 256] = jnp.dot(chosen, gbuf[p, j], preferred_element_type=f32)
        lines = gr_tmp[pl.ds((learner % 8) * 32, 32), :]
        for c in range(8):
            block = lines[:, c * 128 : c * 128 + 128]
            gs32[c, p] = block
            gs[c, p] = block.astype(bf16)

    @pl.loop(1, NG)
    def _(k):
        to = (g + k) % NG
        remote(gs.at[to // 2], gr.at[k - 1], pair_send.at[4], pair_recv.at[4], (d, t, to)).start()

    finish(0)
    finish(1)
    spread_on(rows_at, rows_half, 1)

    own_rows_ready()
    left(0)
    left(1)

    many(gr, 4).wait_recv()
    for p in range(2):
        total = gs32[g // 2, p]
        for k in range(NG - 1):
            total = total + gr[k, p].astype(f32)
        gram_right[p] = jnp.where(g % 2 == 0, total[:, :64], total[:, 64:])

    for p in range(2):
        total = uf[p, pl.ds(t * 16, 16), :]
        for k in (1, 3, 2):
            here = ur.at[p, k - 1]
            remote(here, here, x_send.at[6 + p, k], x_recv.at[6 + p, k], (d, sibling, g)).wait_recv()
            total = total + ur[p, k - 1]
        update[p] = total

    for store in stores:
        store.wait()
    for copy in sent:
        copy.wait_send()
    many(gr, 4).wait_send()

    @pl.when(mine)
    def _():
        many(r2.at[pl.ds(0, 15)], 1).wait_send()

    @pl.when(jnp.logical_not(mine))
    def _():
        many(r2, 1).wait_send()

    @pl.when(y == t)
    def _():
        for k in (2, 1, 3):
            remote(right_root, own_root(x), rr_send.at[k], rr_recv.at[0], (d, sibling, g)).wait_send()


def outputs(left_stat, gram_left, right_stat, gram_right, momentum, update, new_left, new_right, new_momentum):
    new_left[...] = stat_decay * left_stat[...] + (1.0 - stat_decay) * gram_left[...]
    new_right[...] = stat_decay * right_stat[...] + (1.0 - stat_decay) * gram_right[...]
    new_momentum[...] = momentum_decay * momentum[...] + update[...]


def shards(tokens, cotangents, left_stat, right_stat, left_root, right_root, momentum):
    vmem = pl.BlockSpec(memory_space=pltpu.VMEM)
    V, S = pltpu.VMEM, pltpu.SemaphoreType.DMA
    gram_left, gram_right, update = pl.pallas_call(
        kernel,
        out_shape=(
            jax.ShapeDtypeStruct((2, 256, 512), f32),
            jax.ShapeDtypeStruct((2, 32, 64), f32),
            jax.ShapeDtypeStruct((2, 16, 1024), f32),
        ),
        in_specs=[pl.BlockSpec(memory_space=pltpu.HBM)] * 4,
        out_specs=(pl.BlockSpec(memory_space=pltpu.HBM), vmem, vmem),
        scratch_shapes=[
            V(tokens.shape, bf16),
            V(cotangents.shape, bf16),
            V((2, NT, 256, 512), bf16),
            V(right_root.shape, bf16),
            V((NZ, 2, 64, 256), f32),
            V((2, 4, 4, 32, 256), f32),
            V((2, NT, 512, 256), bf16),
            V((NG, 16, 128), bf16),
            V((16, 16, 128), bf16),
            V((NX, NY, 16, 16, 128), bf16),
            V((2, NT, 256, 256), bf16),
            V((2, 256, 1024), bf16),
            V((2, 3, 256, 256), bf16),
            V((2, 3, 256, 256), bf16),
            V((2, 256, 256), f32),
            V((2, 3, 64, 256), bf16),
            V((2, 3, 64, 256), bf16),
            V((2, 64, 1024), f32),
            V((2, 3, 16, 1024), f32),
            V((256, 1024), f32),
            V((8, 2, 32, 128), f32),
            V((8, 2, 32, 128), bf16),
            V((NG - 1, 2, 32, 128), bf16),
            V((2, 256, 512), f32),
            S((2, 4, 4)), S((2, 4, 4)),
            S((2, 8)), S((2, 8)),
            S((8,)), S((8,)),
            S((8,)), S((8,)),
            S((8,)), S((8,)),
            S((9, 4)), S((9, 4)),
            S((5,)), S((5,)),
            S((6,)),
            S((3,)), S((3,)),
            S((4,)), S((1,)),
        ],
        compiler_params=pltpu.CompilerParams(
            collective_id=0, has_side_effects=True, vmem_limit_bytes=60 * 1024 * 1024
        ),
    )(tokens, cotangents, left_root, right_root)
    arrays = (left_stat, gram_left, right_stat, gram_right, momentum, update)
    blocks = [pl.BlockSpec((1, *array.shape[1:]), lambda p: (p, 0, 0)) for array in arrays]
    return pl.pallas_call(
        outputs,
        grid=(2,),
        out_shape=tuple(jax.ShapeDtypeStruct(array.shape, f32) for array in arrays[::2]),
        in_specs=blocks,
        out_specs=tuple(blocks[::2]),
        name="outputs",
    )(*arrays)


def solution(mesh):
    return jax.shard_map(
        shards,
        mesh=mesh,
        in_specs=(
            P("dp", "grid"),
            P(None, "dp", "tensor"),
            P(None, ("dp", "tensor"), "grid"),
            P(None, ("dp", "tensor"), "grid"),
            P(None, ("dp", "tensor"), "grid"),
            P(None, "grid", None),
            P(None, ("dp", "tensor", "grid"), None),
        ),
        out_specs=(
            P(None, ("dp", "tensor"), "grid"),
            P(None, ("dp", "tensor"), "grid"),
            P(None, ("dp", "tensor", "grid"), None),
        ),
        check_vma=False,
    )
```
